32 devices in a mesh: pop: 4 (over x, core), fsdp: 8 (over z, y).
Axes of the slice: x: 2, y: 2, z: 4, core: 2. Of those that a mesh axis runs over, the one named last changes fastest.
Arguments:
- tokens: bfloat16 [512, 5120], P('pop', 'fsdp'), may hold values from -6 to 6
- seeds: int32 [512], replicated, may hold values from 0 to 1048575
- fitness: float32 [512], P(('pop', 'fsdp')), may hold values from -60 to 60
- gate_weight: bfloat16 [5120, 14336], P('fsdp', 'pop'), may hold values from -0.078125 to 0.078125
- up_weight: bfloat16 [5120, 14336], P('fsdp', 'pop'), may hold values from -0.078125 to 0.078125
- gate_first: float32 [5120, 14336], P('fsdp', 'pop'), may hold values from -4 to 4
- up_first: float32 [5120, 14336], P('fsdp', 'pop'), may hold values from -4 to 4
- gate_second: float32 [5120, 14336], P('fsdp', 'pop'), may hold values from 0.05 to 2
- up_second: float32 [5120, 14336], P('fsdp', 'pop'), may hold values from 0.05 to 2
Outputs:
- hidden: bfloat16 [512, 14336], P('fsdp', 'pop')
- gate_new: bfloat16 [5120, 14336], P('fsdp', 'pop')
- up_new: bfloat16 [5120, 14336], P('fsdp', 'pop')
- gate_first_new: float32 [5120, 14336], P('fsdp', 'pop')
- up_first_new: float32 [5120, 14336], P('fsdp', 'pop')
- gate_second_new: float32 [5120, 14336], P('fsdp', 'pop')
- up_second_new: float32 [5120, 14336], P('fsdp', 'pop')
The draws below stay inside these ranges and needn't reach their ends.
All inputs are finite; a program needn't handle non-finite values.
Results may differ from the reference program's by a relative error of at most 0.0022.
Values may be sent and summed in bfloat16 or wider, within the bound.
No kernel may reach another device: no remote copies, remote signals or barrier semaphores. Data moves between devices by JAX's collectives and lax.ppermute only.
A program may use at most 192 MiB of HBM per device.

```python
import math
import jax
import jax.numpy as jnp
from jax import lax

D = 5120
FW = 14336
MEMBERS = 512


def draw_fitness(key, part):
    order = jnp.arange(MEMBERS, dtype=jnp.float32) / (MEMBERS - 1)
    noise = jax.random.truncated_normal(jax.random.fold_in(key, 23), -4.0, 4.0, (MEMBERS,), jnp.float32)
    spread = jnp.exp(order * math.log(10.0))
    return (spread * noise + 0.5 + 1.5 * order).astype(jnp.float32)


def plant(entries, stream_key, smallest, top_value):
    longest = entries.shape.index(max(entries.shape))
    spots = []
    for shift in (0, 1):
        where = [jax.random.randint(jax.random.fold_in(stream_key, axis), (), 0, length) for axis, length in enumerate(entries.shape)]
        where[longest] = (where[longest] + shift) % entries.shape[longest]
        spots.append(tuple(where))
    return entries.at[spots[0]].set(smallest).at[spots[1]].set(top_value)


def shard_levels(rng, shape, pieces, smallest, high):
    factor_of = 1.0
    for axis_at, parts in pieces:
        steps = jax.random.uniform(jax.random.fold_in(jax.random.fold_in(rng, 6), axis_at), (parts,), jnp.float32, smallest / len(pieces), high / len(pieces))
        factor_of = factor_of * jnp.repeat(jnp.exp(steps), shape[axis_at] // parts).reshape((-1,) + (1,) * (len(shape) - 1 - axis_at))
    return factor_of


def scatter_about(key, dims, scale, most, cuts=(), held_as=jnp.bfloat16):
    drawn = jax.random.normal(key, dims, jnp.float32) * scale
    if len(cuts) > 0:
        drawn = shard_levels(key, dims, cuts, -0.22, 0.18) * drawn
    return jnp.clip(drawn, min=-most, max=most).astype(held_as)


def setup_inputs(seed: int = 0) -> dict:
    key_list = jax.random.split(jax.random.key(seed), 10)
    return {
        "tokens": scatter_about(key_list[0], (MEMBERS, D), 1.0, 6.0, ((0, 4), (1, 8))),
        "seeds": plant(jax.random.randint(key_list[1], (MEMBERS,), 0, 1048576), jax.random.fold_in(key_list[1], 1), 0, 1048575).astype(jnp.int32),
        "fitness": draw_fitness(jax.random.fold_in(key_list[9], 71), 0),
        "gate_weight": scatter_about(key_list[3], (D, FW), D ** -0.5, 0.078125, ((0, 8), (1, 4))),
        "up_weight": scatter_about(key_list[4], (D, FW), D ** -0.5, 0.078125, ((0, 8), (1, 4))),
        "gate_first": scatter_about(key_list[5], (D, FW), 0.5, 4.0, ((0, 8), (1, 4)), jnp.float32),
        "up_first": scatter_about(key_list[6], (D, FW), 0.5, 4.0, ((0, 8), (1, 4)), jnp.float32),
        "gate_second": jnp.clip(jnp.exp(math.log(2.0) - 3.6888794 * jax.random.uniform(key_list[7], (D, FW), jnp.float32) ** shard_levels(key_list[7], (D, FW), ((0, 8), (1, 4)), -0.2, 0.2)), 0.05, 2.0),
        "up_second": jnp.clip(jnp.exp(math.log(2.0) - 3.6888794 * jax.random.uniform(key_list[8], (D, FW), jnp.float32) ** shard_levels(key_list[8], (D, FW), ((0, 8), (1, 4)), -0.2, 0.2)), 0.05, 2.0),
    }


noise_scale = 0.01
learn_rate = 0.002
beta_first = 0.9
beta_second = 0.99
adam_floor = 1e-08
stat_epsilon = 1e-06

def factor_block(seeds, start, count, salt):
    columns = jnp.arange(count, dtype=jnp.int32) + start
    mixed = seeds[:, None] * 1103515245 + columns[None, :] * 40503 + salt * 7919
    mixed = jnp.bitwise_xor(mixed, jnp.right_shift(mixed, 15))
    mixed = mixed * 73244475
    mixed = jnp.bitwise_xor(mixed, jnp.right_shift(mixed, 13))
    level = jnp.bitwise_and(mixed, 255)
    return ((2 * level - 255).astype(jnp.float32) * (1.0 / 256.0)).astype(jnp.bfloat16)

def perturbed(tokens, weight, left, right):
    base = jnp.dot(tokens, weight, preferred_element_type=jnp.float32)
    along = lax.optimization_barrier(jnp.sum(tokens.astype(jnp.float32) * left.astype(jnp.float32), axis=1))
    return base + noise_scale * along[:, None] * right.astype(jnp.float32)

def gradient(scaled, left, right):
    weighted = (scaled[:, None] * right.astype(jnp.float32)).astype(jnp.bfloat16)
    total = lax.dot_general(left, weighted, (((0,), (0,)), ((), ())), preferred_element_type=jnp.float32)
    return total * (1.0 / (left.shape[0] * noise_scale))

def adam_step(weight, first, second, grad):
    first_new = beta_first * first + (1.0 - beta_first) * grad
    second_new = beta_second * second + (1.0 - beta_second) * grad * grad
    moved = weight.astype(jnp.float32) + learn_rate * first_new / (jnp.sqrt(second_new) + adam_floor)
    return (moved.astype(jnp.bfloat16), first_new, second_new)

def reference(tokens, seeds, fitness, gate_weight, up_weight, gate_first, up_first, gate_second, up_second):
    left_gate = factor_block(seeds, 0, D, 1)
    right_gate = factor_block(seeds, 0, FW, 2)
    left_up = factor_block(seeds, 0, D, 3)
    right_up = factor_block(seeds, 0, FW, 4)
    gate = perturbed(tokens, gate_weight, left_gate, right_gate)
    up = perturbed(tokens, up_weight, left_up, right_up)
    hidden = (jax.nn.silu(gate) * up).astype(jnp.bfloat16)
    center = jnp.mean(fitness)
    spread = jnp.mean(jnp.square(fitness - center))
    scaled = (fitness - center) / jnp.sqrt(spread + stat_epsilon)
    grad_gate = gradient(scaled, left_gate, right_gate)
    grad_up = gradient(scaled, left_up, right_up)
    gate_new, gate_first_new, gate_second_new = adam_step(gate_weight, gate_first, gate_second, grad_gate)
    up_new, up_first_new, up_second_new = adam_step(up_weight, up_first, up_second, grad_up)
    return (hidden, gate_new, up_new, gate_first_new, up_first_new, gate_second_new, up_second_new)
```

```python
import functools

import jax
import jax.numpy as jnp
from jax import lax
from jax.experimental import pallas as pl
from jax.experimental.pallas import tpu as pltpu
from jax.sharding import PartitionSpec as P

noise_scale = 0.01
learn_rate = 0.002
beta_first = 0.9
beta_second = 0.99
adam_floor = 1e-08
stat_epsilon = 1e-06

f32 = jnp.float32
bf16 = jnp.bfloat16
wire = jnp.float16


def mixed_levels(mixed):
    mixed = jnp.bitwise_xor(mixed, jnp.right_shift(mixed, 15))
    mixed = mixed * 73244475
    mixed = jnp.bitwise_xor(mixed, jnp.right_shift(mixed, 13))
    level = jnp.bitwise_and(mixed, 255)
    return (2 * level - 255).astype(f32) * (1.0 / 256.0)


def member_part(seeds):
    return seeds * 1103515245


def column_part(columns, salt):
    return columns * 40503 + salt * 7919


def factor_levels(seed, column, salt):
    return mixed_levels(member_part(seed) + column_part(column, salt))


def factor_block(seeds, start, count, salt):
    columns = jnp.arange(count, dtype=jnp.int32) + start
    return factor_levels(seeds[:, None], columns[None, :], salt)


def factor_block_turned(seeds, start, count, salt):
    columns = jnp.arange(count, dtype=jnp.int32) + start
    return factor_levels(seeds[None, :], columns[:, None], salt).astype(bf16)


def adam_kernel(scale, row_tile, extra, *refs):
    left, member, unit, scaled, kept_tokens, weight, first, second = refs[:8]
    weight_new, first_new, second_new, kept = refs[8 + extra :]
    weighted = (scaled[...] * mixed_levels(member[...] + unit[...])).astype(bf16)
    kept[...] = jnp.dot(kept_tokens[...], weight[...], preferred_element_type=f32)
    for start in range(0, left.shape[0], row_tile):
        rows = slice(start, start + row_tile)
        g = jnp.dot(left[rows, :], weighted, preferred_element_type=f32) * scale
        f = beta_first * first[rows, :] + (1.0 - beta_first) * g
        s = beta_second * second[rows, :] + (1.0 - beta_second) * g * g
        first_new[rows, :] = f
        second_new[rows, :] = s
        moved = weight[rows, :].astype(f32) + learn_rate * f / (jnp.sqrt(s) + adam_floor)
        weight_new[rows, :] = moved.astype(bf16)


def adam_part(left, member, unit, scaled, kept_tokens, weight, first, second, before, start, tile, steps):
    width, units = weight.shape
    members = member.shape[0]
    row_tile = 128 if width % 128 == 0 else width
    kept_rows = kept_tokens.shape[0]
    base = start // tile
    full = lambda dtype: jax.ShapeDtypeStruct((width, units), dtype)
    big = lambda: pl.BlockSpec((width, tile), lambda j: (0, base + j))
    in_specs = [
        pl.BlockSpec((width, members), lambda j: (0, 0)),
        pl.BlockSpec((members, 1), lambda j: (0, 0)),
        pl.BlockSpec((1, tile), lambda j: (0, base + j)),
        pl.BlockSpec((members, 1), lambda j: (0, 0)),
        pl.BlockSpec((kept_rows, width), lambda j: (0, 0)),
        big(),
        big(),
        big(),
    ]
    args = [left, member, unit, scaled, kept_tokens, weight, first, second]
    aliases = {}
    if before is not None:
        args += list(before)
        aliases = {8: 0, 9: 1, 10: 2}
    extra = len(args) - 8
    in_specs += [pl.BlockSpec(memory_space=pl.ANY)] * extra
    return pl.pallas_call(
        functools.partial(adam_kernel, 1.0 / (members * noise_scale), row_tile, extra),
        grid=(steps,),
        in_specs=in_specs,
        out_specs=[big(), big(), big(), pl.BlockSpec((kept_rows, tile), lambda j: (0, j))],
        out_shape=[
            full(bf16),
            full(f32),
            full(f32),
            jax.ShapeDtypeStruct((kept_rows, tile * steps), f32),
        ],
        input_output_aliases=aliases,
        compiler_params=pltpu.CompilerParams(vmem_limit_bytes=50 * 1024 * 1024),
        cost_estimate=pl.CostEstimate(
            flops=2 * width * tile * steps * (members + kept_rows),
            bytes_accessed=20 * width * tile * steps,
            transcendentals=0,
        ),
    )(*args)


def sort_kernel(orders, share, index, seeds, columns, *refs):
    kinds = len(orders)
    pieces = refs[: -3 * kinds - 1]
    turned, alongs, ids = (refs[len(pieces) + i * kinds :][:kinds] for i in range(3))
    held = refs[-1]
    per_piece = pieces[0].shape[0] // share
    for p, piece in enumerate(pieces):
        for k in range(per_piece):
            held[p * per_piece + k] = piece[k * share : (k + 1) * share, :]
    for mask in range(held.shape[0]):
        rows = held[index[0, mask]]
        block = pl.multiple_of(index[1, mask] * share, share)
        member = member_part(seeds[pl.ds(block, share), :])
        wide = rows.astype(f32)
        along = [
            noise_scale
            * jnp.sum(wide * mixed_levels(member + columns[i : i + 1, :]), axis=1, keepdims=True)
            for i in range(2)
        ]
        for kind, order in enumerate(orders):
            at = order.index(mask) * share
            turned[kind][at : at + share, :] = rows
            ids[kind][at : at + share, :] = member
            for i in range(2):
                alongs[kind][at : at + share, i : i + 1] = along[i]


def sort_blocks(pieces, index, seeds, columns, orders):
    members = seeds.shape[0]
    width = pieces[0].shape[1]
    shares = len(orders[0])
    share = members // shares
    kinds = len(orders)
    whole = pl.BlockSpec(memory_space=pltpu.VMEM)
    outs = pl.pallas_call(
        functools.partial(sort_kernel, orders, share),
        in_specs=[pl.BlockSpec(memory_space=pltpu.SMEM)] + [whole] * (2 + len(pieces)),
        out_specs=[whole] * (3 * kinds),
        out_shape=[jax.ShapeDtypeStruct((members, width), bf16)] * kinds
        + [jax.ShapeDtypeStruct((members, 2), f32)] * kinds
        + [jax.ShapeDtypeStruct((members, 1), jnp.int32)] * kinds,
        scratch_shapes=[pltpu.VMEM((shares, share, width), bf16)],
        compiler_params=pltpu.CompilerParams(vmem_limit_bytes=32 * 1024 * 1024),
    )(index, seeds[:, None], columns, *pieces)
    return outs[:kinds], outs[kinds : 2 * kinds], outs[2 * kinds :]


def block_order(bits):
    order = [0]
    for bit in reversed(bits):
        order = order + [mask ^ (1 << bit) for mask in order]
    return order


def shards(
    tokens, seeds, fitness, gate_weight, up_weight, gate_first, up_first, gate_second, up_second
):
    members = seeds.shape[0]
    width_part, unit_part = gate_weight.shape
    shares = lax.axis_size("fsdp")
    share = members // shares
    me = lax.axis_index("fsdp")
    width_start = me * width_part
    unit_start = lax.axis_index("pop") * unit_part
    levels = shares.bit_length() - 1
    across = list(range(levels))
    along_first = [1, 0] + across[2:] if levels > 1 else across

    def exchange(x, bit, axis="fsdp"):
        size = lax.axis_size(axis)
        return lax.ppermute(x, axis, [(i, i ^ (1 << bit)) for i in range(size)])

    def after(x, *others):
        return lax.optimization_barrier((x, others))[0]

    pops = lax.axis_size("pop")
    pop = lax.axis_index("pop")
    per_pop = shares // pops
    pieces = [tokens]
    for mask in reversed(range(1, pops)):
        pieces.insert(1, lax.ppermute(tokens, "pop", [(i, i ^ mask) for i in range(pops)]))

    fit = lax.dynamic_update_slice(
        jnp.zeros((members,), f32), fitness, ((pop * shares + me) * fitness.shape[0],)
    )
    turned_gate = factor_block_turned(seeds, width_start, width_part, 1)
    for bit in range(levels):
        fit = fit + exchange(fit, bit)
        if bit == 0:
            turned_up = factor_block_turned(after(seeds, fit), width_start, width_part, 3)

    masks = jnp.arange(shares)
    blocks = jnp.bitwise_xor(me, masks)
    slots = jnp.bitwise_xor(blocks // per_pop, pop) * per_pop + blocks % per_pop
    features = jnp.arange(width_part, dtype=jnp.int32) + width_start
    orders = [block_order(across), block_order(along_first)]
    bits_of = [across, along_first]
    tokens_of, along_of, member_of = sort_blocks(
        pieces,
        jnp.stack([slots, blocks]).astype(jnp.int32),
        seeds,
        jnp.stack([column_part(features, 1), column_part(features, 3)]),
        orders,
    )

    fit = after(fit, *tokens_of)
    for bit in range(pops.bit_length() - 1):
        fit = fit + exchange(fit, bit, "pop")
    all_fitness = fit

    columns = jnp.arange(unit_part, dtype=jnp.int32) + unit_start
    member = member_part(seeds)[:, None]

    center = jnp.mean(all_fitness)
    spread = jnp.mean(jnp.square(all_fitness - center))
    scaled = ((all_fitness - center) / jnp.sqrt(spread + stat_epsilon))[:, None]

    parts = 2
    tile = unit_part // parts
    per_call = 2 if tile % 256 == 0 else 1
    half = members // 2
    plan = [(0, "gate", 1), (0, "up", 0), (1, "gate", 0), (1, "up", 0)]
    state = {
        "gate": (turned_gate, column_part(columns, 2)[None, :], gate_weight, gate_first, gate_second),
        "up": (turned_up, column_part(columns, 4)[None, :], up_weight, up_first, up_second),
    }

    def term(name, kind, at, rows):
        along = along_of[kind][rows, {"gate": 0, "up": 1}[name]][:, None]
        unit = state[name][1][:, at * tile : (at + 1) * tile]
        return along * mixed_levels(member_of[kind][rows] + unit)

    sent = []
    for at, name, kind in plan:
        weight = state[name][2][:, at * tile : (at + 1) * tile]
        rows = tokens_of[kind][half:]
        if sent:
            rows = after(rows, partial)
        partial = jnp.dot(rows, weight, preferred_element_type=f32)
        partial = (partial + term(name, kind, at, slice(half, None))).astype(wire)
        sent.append(exchange(partial, bits_of[kind][0]))

    updated = {"gate": None, "up": None}
    kept_of = {}

    summed = {}
    running = {}

    def update(index, before=(), held=()):
        at, name, kind = plan[index]
        left, unit, weight, first, second = state[name]
        tied, _ = lax.optimization_barrier((scaled, list(before)))
        *done, kept = adam_part(
            left,
            member,
            unit,
            tied,
            tokens_of[kind][:half],
            weight,
            first,
            second,
            updated[name],
            at * tile,
            tile // per_call,
            per_call,
        )
        updated[name] = done
        kept_of[at, name] = kept
        for other in held:
            running[other] = after(running[other], kept)


    def reduce_step(index, level):
        at, name, kind = plan[index]
        if level == 0:
            kept = kept_of[at, name]
            running[index] = [kept, after(sent[index], kept)]
        *summands, arrived = running[index]
        rows = arrived.shape[0] // 2

        def added(part):
            total = summands[0][part]
            if level == 0:
                total = total + term(name, kind, at, part)
            for x in summands[1:] + [arrived]:
                total = total + x[part].astype(f32)
            return total

        if level == levels - 1:
            summed[name, at] = added(slice(None))
            return None
        outgoing = added(slice(rows, 2 * rows)).astype(wire)
        running[index] = [added(slice(0, rows)), exchange(outgoing, bits_of[kind][level + 1])]
        return outgoing

    update(0)
    update(1)
    out_0 = reduce_step(0, 0)
    out_1 = reduce_step(1, 0)
    update(2, [out_0, out_1])
    out_2 = reduce_step(2, 0)
    out_3 = reduce_step(1, 1)
    update(3, [out_2, out_3], [0, 2])
    out_4 = reduce_step(3, 0)
    for index in (0, 2):
        running[index] = after(running[index], out_4)
    reduce_step(0, 1)
    reduce_step(2, 1)
    reduce_step(3, 1)
    for index in range(len(plan)):
        for level in range(2, levels):
            reduce_step(index, level)

    def finished(name):
        return jnp.concatenate([summed[name, at] for at in range(parts)], axis=1)

    hidden = (jax.nn.silu(finished("gate")) * finished("up")).astype(bf16)
    gate_new, gate_first_new, gate_second_new = updated["gate"]
    up_new, up_first_new, up_second_new = updated["up"]
    return (hidden, gate_new, up_new, gate_first_new, up_first_new, gate_second_new, up_second_new)


def solution(mesh):
    placed = (P("pop", "fsdp"), P(), P(("pop", "fsdp"))) + (P("fsdp", "pop"),) * 6
    return jax.shard_map(
        shards,
        mesh=mesh,
        in_specs=placed,
        out_specs=(P("fsdp", "pop"),) * 7,
        check_vma=False,
    )
```

```python
import functools

import jax
import jax.numpy as jnp
from jax import lax
from jax.experimental import pallas as pl
from jax.experimental.pallas import tpu as pltpu
from jax.sharding import PartitionSpec as P

noise_scale = 0.01
learn_rate = 0.002
beta_first = 0.9
beta_second = 0.99
adam_floor = 1e-08
stat_epsilon = 1e-06

f32 = jnp.float32
bf16 = jnp.bfloat16
wire = jnp.float16


def mixed_levels(mixed):
    mixed = jnp.bitwise_xor(mixed, jnp.right_shift(mixed, 15))
    mixed = mixed * 73244475
    mixed = jnp.bitwise_xor(mixed, jnp.right_shift(mixed, 13))
    level = jnp.bitwise_and(mixed, 255)
    return level.astype(f32) * (2.0 / 256.0) - 255.0 / 256.0


def member_part(seeds):
    return seeds * 1103515245


def column_part(columns, salt):
    return columns * 40503 + salt * 7919


def factor_levels(seed, column, salt):
    return mixed_levels(member_part(seed) + column_part(column, salt))


def factor_block(seeds, start, count, salt):
    columns = jnp.arange(count, dtype=jnp.int32) + start
    return factor_levels(seeds[:, None], columns[None, :], salt)


def factor_block_turned(seeds, start, count, salt):
    columns = jnp.arange(count, dtype=jnp.int32) + start
    return factor_levels(seeds[None, :], columns[:, None], salt).astype(bf16)


def adam_kernel(scale, row_tile, keeps, extra, *refs):
    left, member, unit, scaled, weight, first, second = refs[:7]
    if keeps:
        tokens, along, kept_member = refs[7:10]
    outs = refs[7 + 3 * keeps + extra :]
    weight_new, first_new, second_new, tick = outs[:4]
    tick[...] = jnp.zeros_like(tick)
    weighted = (scaled[...] * mixed_levels(member[...] + unit[...])).astype(bf16)
    if keeps:
        product = jnp.dot(tokens[...], weight[...], preferred_element_type=f32)
        outs[4][...] = product + along[...] * mixed_levels(kept_member[...] + unit[...])
    for start in range(0, left.shape[0], row_tile):
        rows = slice(start, start + row_tile)
        g = jnp.dot(left[rows, :], weighted, preferred_element_type=f32)
        f = beta_first * first[rows, :] + ((1.0 - beta_first) * scale) * g
        s = beta_second * second[rows, :] + ((1.0 - beta_second) * scale * scale) * g * g
        first_new[rows, :] = f
        second_new[rows, :] = s
        floor = s * lax.rsqrt(s) + adam_floor
        inverse = pl.reciprocal(floor, approx=True)
        inverse = inverse * (2.0 - floor * inverse)
        moved = weight[rows, :].astype(f32) + (learn_rate * f) * inverse
        weight_new[rows, :] = moved.astype(bf16)


def adam_part(left, member, unit, scaled, weight, first, second, kept_from, before, wait_for, start, size):
    width, units = weight.shape
    members = member.shape[0]
    tile = max(t for t in range(128, 1281, 128) if size % t == 0 and start % t == 0)
    base = start // tile
    keeps = kept_from is not None
    full = lambda dtype: jax.ShapeDtypeStruct((width, units), dtype)
    big = lambda: pl.BlockSpec((width, tile), lambda j: (0, base + j))
    fixed = lambda x: pl.BlockSpec(x.shape, lambda j: (0, 0))
    in_specs = [
        fixed(left),
        fixed(member),
        pl.BlockSpec((1, tile), lambda j: (0, base + j)),
        fixed(scaled),
        big(),
        big(),
        big(),
    ]
    args = [left, member, unit, scaled, weight, first, second]
    out_specs = [big(), big(), big(), pl.BlockSpec((1, 1), lambda j: (0, 0))]
    out_shape = [full(bf16), full(f32), full(f32), jax.ShapeDtypeStruct((1, 1), f32)]
    kept_rows = 0
    if keeps:
        kept_rows = kept_from[0].shape[0]
        in_specs += [fixed(x) for x in kept_from]
        args += list(kept_from)
        out_specs.append(pl.BlockSpec((kept_rows, tile), lambda j: (0, j)))
        out_shape.append(jax.ShapeDtypeStruct((kept_rows, size), f32))
    aliases = {}
    if before is not None:
        aliases = {len(args) + i: i for i in range(len(before))}
        args += list(before)
    args += list(wait_for)
    extra = len(args) - len(in_specs)
    in_specs += [pl.BlockSpec(memory_space=pl.ANY)] * extra
    return pl.pallas_call(
        functools.partial(adam_kernel, 1.0 / (members * noise_scale), width // 2, keeps, extra),
        grid=(size // tile,),
        in_specs=in_specs,
        out_specs=out_specs,
        out_shape=out_shape,
        input_output_aliases=aliases,
        compiler_params=pltpu.CompilerParams(vmem_limit_bytes=44 * 1024 * 1024),
        cost_estimate=pl.CostEstimate(
            flops=2 * width * size * (members + kept_rows),
            bytes_accessed=20 * width * size,
            transcendentals=0,
        ),
    )(*args)


def sort_kernel(orders, share, index, seeds, columns, *refs):
    kinds = len(orders)
    pieces = refs[: -3 * kinds - 1]
    turned, alongs, ids = (refs[len(pieces) + i * kinds :][:kinds] for i in range(3))
    held = refs[-1]
    per_piece = pieces[0].shape[0] // share
    for p, piece in enumerate(pieces):
        for k in range(per_piece):
            held[p * per_piece + k] = piece[k * share : (k + 1) * share, :]
    for mask in range(held.shape[0]):
        rows = held[index[0, mask]]
        block = pl.multiple_of(index[1, mask] * share, share)
        member = member_part(seeds[pl.ds(block, share), :])
        wide = rows.astype(f32)
        along = [
            noise_scale
            * jnp.sum(wide * mixed_levels(member + columns[i : i + 1, :]), axis=1, keepdims=True)
            for i in range(2)
        ]
        for kind, order in enumerate(orders):
            at = order.index(mask) * share
            turned[kind][at : at + share, :] = rows
            ids[kind][at : at + share, :] = member
            for i in range(2):
                alongs[kind][at : at + share, i : i + 1] = along[i]


def sort_blocks(pieces, index, seeds, columns, orders):
    members = seeds.shape[0]
    width = pieces[0].shape[1]
    shares = len(orders[0])
    share = members // shares
    kinds = len(orders)
    whole = pl.BlockSpec(memory_space=pltpu.VMEM)
    outs = pl.pallas_call(
        functools.partial(sort_kernel, orders, share),
        in_specs=[pl.BlockSpec(memory_space=pltpu.SMEM)] + [whole] * (2 + len(pieces)),
        out_specs=[whole] * (3 * kinds),
        out_shape=[jax.ShapeDtypeStruct((members, width), bf16)] * kinds
        + [jax.ShapeDtypeStruct((members, 2), f32)] * kinds
        + [jax.ShapeDtypeStruct((members, 1), jnp.int32)] * kinds,
        scratch_shapes=[pltpu.VMEM((shares, share, width), bf16)],
        compiler_params=pltpu.CompilerParams(vmem_limit_bytes=32 * 1024 * 1024),
    )(index, seeds[:, None], columns, *pieces)
    return outs[:kinds], outs[kinds : 2 * kinds], outs[2 * kinds :]


def block_order(bits):
    order = [0]
    for bit in reversed(bits):
        order = order + [mask ^ (1 << bit) for mask in order]
    return order


def shards(
    tokens, seeds, fitness, gate_weight, up_weight, gate_first, up_first, gate_second, up_second
):
    members = seeds.shape[0]
    width_part, unit_part = gate_weight.shape
    shares = lax.axis_size("fsdp")
    share = members // shares
    me = lax.axis_index("fsdp")
    width_start = me * width_part
    unit_start = lax.axis_index("pop") * unit_part
    levels = shares.bit_length() - 1
    across = list(range(levels))
    along_first = [1, 0] + across[2:] if levels > 1 else across

    def exchange(x, mask, axis="fsdp"):
        size = lax.axis_size(axis)
        return lax.ppermute(x, axis, [(i, i ^ mask) for i in range(size)])

    pops = lax.axis_size("pop")
    pop = lax.axis_index("pop")
    per_pop = shares // pops
    pieces = [tokens]
    for mask in reversed(range(1, pops)):
        pieces.insert(1, exchange(tokens, mask, "pop"))

    group = members // fitness.shape[0]
    own = jnp.arange(group)[:, None] == pop * shares + me
    fit = jnp.where(own, fitness[None, :], 0.0)
    turned_gate = factor_block_turned(seeds, width_start, width_part, 1)
    fit = fit + exchange(fit, 1)
    turned_up = factor_block_turned(seeds, width_start, width_part, 3)
    for bit in range(1, levels - 1):
        fit = fit + exchange(fit, 1 << bit)

    masks = jnp.arange(shares)
    blocks = jnp.bitwise_xor(me, masks)
    slots = jnp.bitwise_xor(blocks // per_pop, pop) * per_pop + blocks % per_pop
    features = jnp.arange(width_part, dtype=jnp.int32) + width_start
    orders = [block_order(across), block_order(along_first)]
    bits_of = [across, along_first]
    tokens_of, along_of, member_of = sort_blocks(
        pieces,
        jnp.stack([slots, blocks]).astype(jnp.int32),
        seeds,
        jnp.stack([column_part(features, 1), column_part(features, 3)]),
        orders,
    )

    columns = jnp.arange(unit_part, dtype=jnp.int32) + unit_start
    member = member_part(seeds)[:, None]

    half = members // 2
    unit_tiles = unit_part // 128
    cut = {"gate": unit_tiles // 2 * 128, "up": unit_tiles // 2 * 128}
    plan = [("gate", 0, 1), ("up", 0, 0), ("gate", 1, 0), ("up", 1, 1)]

    def span(index):
        name, at, _ = plan[index]
        return (0, cut[name]) if at == 0 else (cut[name], unit_part)

    state = {
        "gate": (turned_gate, column_part(columns, 2)[None, :], gate_weight, gate_first, gate_second),
        "up": (turned_up, column_part(columns, 4)[None, :], up_weight, up_first, up_second),
    }

    def product(index, rows, tick):
        name, _, kind = plan[index]
        start, stop = span(index)
        total = jnp.dot(
            tokens_of[kind][rows], state[name][2][:, start:stop], preferred_element_type=f32
        )
        along = along_of[kind][rows, {"gate": 0, "up": 1}[name]][:, None]
        if tick is not None:
            along = along + tick
        unit = state[name][1][:, start:stop]
        return total + along * mixed_levels(member_of[kind][rows] + unit)

    sent = [None] * len(plan)

    def zero_of(x):
        return x[:1, :1].astype(f32) * 0.0

    def send(index, tick):
        partial = product(index, slice(half, None), tick).astype(wire)
        sent[index] = exchange(partial, 1 << bits_of[plan[index][2]][0])
        return partial

    fit = fit + zero_of(along_of[0])
    if levels > 1:
        fit = fit + exchange(fit, 1 << (levels - 1))
    ready = fit[:1, :1] * 0.0
    wait = [send(1, None), send(0, ready), send(2, ready)]
    wait = [x[:8, :128].astype(f32) for x in wait]
    fit = sum([exchange(fit, mask, "pop") for mask in range(1, pops)], fit)
    center = jnp.mean(fit)
    spread = jnp.mean(jnp.square(fit - center))
    scaled = ((fit - center) / jnp.sqrt(spread + stat_epsilon)).reshape(members, 1)

    updated = {"gate": None, "up": None}
    kept_of = {}
    summed = {}
    running = {}

    def update(index, wait_for=(), keeps=True, piece=0, pieces=1):
        name, _, kind = plan[index]
        left, unit, weight, first, second = state[name]
        start, stop = span(index)
        size = (stop - start) // pieces
        start += piece * size
        kept_from = None
        if keeps:
            side = {"gate": 0, "up": 1}[name]
            kept_from = (
                tokens_of[kind][:half],
                along_of[kind][:half, side : side + 1],
                member_of[kind][:half],
            )
        done = adam_part(
            left,
            member,
            unit,
            scaled,
            weight,
            first,
            second,
            kept_from,
            updated[name],
            wait_for,
            start,
            size,
        )
        updated[name] = done[:3]
        if keeps:
            kept_of[index] = done[4]
        return done[3]

    def reduce_step(index, level, tick):
        if level == 0:
            running[index] = [kept_of[index], sent[index]]
        kept, arrived = running[index]
        rows = arrived.shape[0] // 2
        if level == levels - 1:
            summed[index] = kept + arrived.astype(f32) + tick
            return summed[index]
        added = lambda part: kept[part] + arrived[part].astype(f32) + tick
        outgoing = added(slice(rows, 2 * rows)).astype(wire)
        bit = bits_of[plan[index][2]][level + 1]
        running[index] = [added(slice(0, rows)), exchange(outgoing, 1 << bit)]
        return running[index][0]

    tick = update(0, wait)
    wait = [reduce_step(0, 0, tick)]
    kept_of[1] = product(1, slice(0, half), tick)
    wait += [reduce_step(1, 0, tick), send(3, tick)[:8, :128].astype(f32)]
    tick = update(1, wait, keeps=False)
    wait = [reduce_step(1, 1, tick), reduce_step(0, 1, tick)]
    for index in (2, 3):
        kept_of[index] = product(index, slice(0, half), tick)
        wait.append(reduce_step(index, 0, tick))
    tick = update(2, wait, keeps=False)
    wait = [reduce_step(2, 1, tick), reduce_step(3, 1, tick)]
    tick = update(3, wait, keeps=False)
    for level in range(2, levels):
        for index in (0, 1, 2, 3):
            reduce_step(index, level, tick)

    def finished(name):
        return jnp.concatenate([summed[i] for i in range(len(plan)) if plan[i][0] == name], axis=1)

    hidden = (jax.nn.silu(finished("gate")) * finished("up")).astype(bf16)
    gate_new, gate_first_new, gate_second_new = updated["gate"]
    up_new, up_first_new, up_second_new = updated["up"]
    return (hidden, gate_new, up_new, gate_first_new, up_first_new, gate_second_new, up_second_new)


def solution(mesh):
    placed = (P("pop", "fsdp"), P(), P(("pop", "fsdp"))) + (P("fsdp", "pop"),) * 6
    return jax.shard_map(
        shards,
        mesh=mesh,
        in_specs=placed,
        out_specs=(P("fsdp", "pop"),) * 7,
        check_vma=False,
    )
```

```python
import functools

import jax
import jax.numpy as jnp
from jax import lax
from jax.experimental import pallas as pl
from jax.experimental.pallas import tpu as pltpu
from jax.sharding import PartitionSpec as P

noise_scale = 0.01
learn_rate = 0.002
beta_first = 0.9
beta_second = 0.99
adam_floor = 1e-08
stat_epsilon = 1e-06

f32 = jnp.float32
bf16 = jnp.bfloat16
wire = jnp.float16


def mixed_levels(mixed):
    mixed = jnp.bitwise_xor(mixed, jnp.right_shift(mixed, 15))
    mixed = mixed * 73244475
    mixed = jnp.bitwise_xor(mixed, jnp.right_shift(mixed, 13))
    level = jnp.bitwise_and(mixed, 255)
    return level.astype(f32) * (2.0 / 256.0) - 255.0 / 256.0


def member_part(seeds):
    return seeds * 1103515245


def column_part(columns, salt):
    return columns * 40503 + salt * 7919


def factor_levels(seed, column, salt):
    return mixed_levels(member_part(seed) + column_part(column, salt))


def factor_block(seeds, start, count, salt):
    columns = jnp.arange(count, dtype=jnp.int32) + start
    return factor_levels(seeds[:, None], columns[None, :], salt)


def factor_block_turned(seeds, start, count, salt):
    columns = jnp.arange(count, dtype=jnp.int32) + start
    return factor_levels(seeds[None, :], columns[:, None], salt).astype(bf16)


def adam_kernel(scale, row_tile, extra, *refs):
    left, member, unit, fitness, weight, first, second = refs[:7]
    weight_new, first_new, second_new, tick = refs[7 + extra :]
    tick[...] = jnp.zeros_like(tick)
    members = fitness.shape[0]
    center = jnp.sum(fitness[...], axis=0, keepdims=True) / members
    apart = fitness[...] - center
    spread = jnp.sum(apart * apart, axis=0, keepdims=True) / members
    scaled = apart / jnp.sqrt(spread + stat_epsilon)
    weighted = (scaled * mixed_levels(member[...] + unit[...])).astype(bf16)
    for start in range(0, left.shape[0], row_tile):
        rows = slice(start, start + row_tile)
        g = jnp.dot(left[rows, :], weighted, preferred_element_type=f32)
        f = beta_first * first[rows, :] + ((1.0 - beta_first) * scale) * g
        s = beta_second * second[rows, :] + ((1.0 - beta_second) * scale * scale) * g * g
        first_new[rows, :] = f
        second_new[rows, :] = s
        floor = s * lax.rsqrt(s) + adam_floor
        inverse = pl.reciprocal(floor, approx=True)
        inverse = inverse * (2.0 - floor * inverse)
        moved = weight[rows, :].astype(f32) + (learn_rate * f) * inverse
        weight_new[rows, :] = moved.astype(bf16)


def adam_part(left, member, unit, fitness, weight, first, second, before, wait_for, start, size):
    width, units = weight.shape
    members = member.shape[0]
    tile = max(t for t in range(128, 1281, 128) if size % t == 0 and start % t == 0)
    base = start // tile
    full = lambda dtype: jax.ShapeDtypeStruct((width, units), dtype)
    big = lambda: pl.BlockSpec((width, tile), lambda j: (0, base + j))
    fixed = lambda x: pl.BlockSpec(x.shape, lambda j: (0, 0))
    in_specs = [
        fixed(left),
        fixed(member),
        pl.BlockSpec((1, tile), lambda j: (0, base + j)),
        fixed(fitness),
        big(),
        big(),
        big(),
    ]
    args = [left, member, unit, fitness, weight, first, second]
    out_specs = [big(), big(), big(), pl.BlockSpec((1, 1), lambda j: (0, 0))]
    out_shape = [full(bf16), full(f32), full(f32), jax.ShapeDtypeStruct((1, 1), f32)]
    aliases = {}
    if before is not None:
        aliases = {len(args) + i: i for i in range(len(before))}
        args += list(before)
    args += list(wait_for)
    extra = len(args) - len(in_specs)
    in_specs += [pl.BlockSpec(memory_space=pl.ANY)] * extra
    return pl.pallas_call(
        functools.partial(adam_kernel, 1.0 / (members * noise_scale), width // 2, extra),
        grid=(size // tile,),
        in_specs=in_specs,
        out_specs=out_specs,
        out_shape=out_shape,
        input_output_aliases=aliases,
        compiler_params=pltpu.CompilerParams(vmem_limit_bytes=44 * 1024 * 1024),
        cost_estimate=pl.CostEstimate(
            flops=2 * width * size * members,
            bytes_accessed=20 * width * size,
            transcendentals=0,
        ),
    )(*args)


def sort_kernel(orders, share, index, seeds, columns, *refs):
    kinds = len(orders)
    pieces = refs[: -3 * kinds - 2]
    turned, alongs, ids = (refs[len(pieces) + i * kinds :][:kinds] for i in range(3))
    held = refs[-1]
    refs[-2][...] = jnp.zeros_like(refs[-2])
    per_piece = pieces[0].shape[0] // share
    for p, piece in enumerate(pieces):
        for k in range(per_piece):
            held[p * per_piece + k] = piece[k * share : (k + 1) * share, :]
    for mask in range(held.shape[0]):
        rows = held[index[0, mask]]
        block = pl.multiple_of(index[1, mask] * share, share)
        member = member_part(seeds[pl.ds(block, share), :])
        wide = rows.astype(f32)
        along = [
            noise_scale
            * jnp.sum(wide * mixed_levels(member + columns[i : i + 1, :]), axis=1, keepdims=True)
            for i in range(2)
        ]
        for kind, order in enumerate(orders):
            at = order.index(mask) * share
            turned[kind][at : at + share, :] = rows
            ids[kind][at : at + share, :] = member
            for i in range(2):
                alongs[kind][at : at + share, i : i + 1] = along[i]


def sort_blocks(pieces, index, seeds, columns, orders):
    members = seeds.shape[0]
    width = pieces[0].shape[1]
    shares = len(orders[0])
    share = members // shares
    kinds = len(orders)
    whole = pl.BlockSpec(memory_space=pltpu.VMEM)
    outs = pl.pallas_call(
        functools.partial(sort_kernel, orders, share),
        in_specs=[pl.BlockSpec(memory_space=pltpu.SMEM)] + [whole] * (2 + len(pieces)),
        out_specs=[whole] * (3 * kinds + 1),
        out_shape=[jax.ShapeDtypeStruct((members, width), bf16)] * kinds
        + [jax.ShapeDtypeStruct((members, 2), f32)] * kinds
        + [jax.ShapeDtypeStruct((members, 1), jnp.int32)] * kinds
        + [jax.ShapeDtypeStruct((1, 1), f32)],
        scratch_shapes=[pltpu.VMEM((shares, share, width), bf16)],
        compiler_params=pltpu.CompilerParams(vmem_limit_bytes=32 * 1024 * 1024),
    )(index, seeds[:, None], columns, *pieces)
    return outs[:kinds], outs[kinds : 2 * kinds], outs[2 * kinds : 3 * kinds], outs[-1]


def block_order(bits):
    order = [0]
    for bit in reversed(bits):
        order = order + [mask ^ (1 << bit) for mask in order]
    return order


def shards(
    tokens, seeds, fitness, gate_weight, up_weight, gate_first, up_first, gate_second, up_second
):
    members = seeds.shape[0]
    width_part, unit_part = gate_weight.shape
    shares = lax.axis_size("fsdp")
    share = members // shares
    me = lax.axis_index("fsdp")
    width_start = me * width_part
    unit_start = lax.axis_index("pop") * unit_part
    levels = shares.bit_length() - 1
    across = list(range(levels))
    along_first = [1, 0] + across[2:] if levels > 1 else across

    def exchange(x, mask, axis="fsdp"):
        size = lax.axis_size(axis)
        return lax.ppermute(x, axis, [(i, i ^ mask) for i in range(size)])

    pops = lax.axis_size("pop")
    pop = lax.axis_index("pop")
    per_pop = shares // pops
    pieces = [tokens]
    for mask in reversed(range(1, pops)):
        pieces.insert(1, exchange(tokens, mask, "pop"))

    group = members // fitness.shape[0]
    own = jnp.arange(group)[:, None] == pop * shares + me
    fit = jnp.where(own, fitness[None, :], 0.0)
    turned_gate = factor_block_turned(seeds, width_start, width_part, 1)
    fit = fit + exchange(fit, 1)
    turned_up = factor_block_turned(seeds, width_start, width_part, 3)
    fit = sum([exchange(fit, mask) for mask in range(2, shares, 2)], fit)

    masks = jnp.arange(shares)
    blocks = jnp.bitwise_xor(me, masks)
    slots = jnp.bitwise_xor(blocks // per_pop, pop) * per_pop + blocks % per_pop
    features = jnp.arange(width_part, dtype=jnp.int32) + width_start
    orders = [block_order(across), block_order(along_first)]
    bits_of = [across, along_first]
    tokens_of, along_of, member_of, tick = sort_blocks(
        pieces,
        jnp.stack([slots, blocks]).astype(jnp.int32),
        seeds,
        jnp.stack([column_part(features, 1), column_part(features, 3)]),
        orders,
    )

    columns = jnp.arange(unit_part, dtype=jnp.int32) + unit_start
    member = member_part(seeds)[:, None]

    kept_rows = slice(0, members // 2)
    sent_rows = slice(members // 2, members)
    unit_tiles = unit_part // 128
    cut = unit_tiles // 2 * 128
    plan = [("gate", 0, 1), ("up", 0, 0), ("gate", 1, 0), ("up", 1, 1)]

    def span(index):
        return (0, cut) if plan[index][1] == 0 else (cut, unit_part)

    state = {
        "gate": (turned_gate, column_part(columns, 2)[None, :], gate_weight, gate_first, gate_second),
        "up": (turned_up, column_part(columns, 4)[None, :], up_weight, up_first, up_second),
    }

    def product(index, rows, tick):
        name, _, kind = plan[index]
        start, stop = span(index)
        total = jnp.dot(
            tokens_of[kind][rows], state[name][2][:, start:stop], preferred_element_type=f32
        )
        along = along_of[kind][rows, {"gate": 0, "up": 1}[name]][:, None]
        unit = state[name][1][:, start:stop]
        return total + along * mixed_levels(member_of[kind][rows] + unit) + tick

    sent = [None] * len(plan)

    def zero_of(x):
        return x[:1, :1] * 0.0

    def send(index, tick):
        partial = product(index, sent_rows, tick).astype(wire)
        sent[index] = exchange(partial, 1 << bits_of[plan[index][2]][0])
        return partial

    fit = fit + tick
    fit = sum([exchange(fit, mask, "pop") for mask in range(1, pops)], fit).reshape(members, 1)
    wait = [send(index, tick)[:8, :128].astype(f32) for index in (0, 1)]

    updated = {"gate": None, "up": None}
    running = {}

    def update(index, wait_for=()):
        name = plan[index][0]
        left, unit, weight, first, second = state[name]
        start, stop = span(index)
        *updated[name], tick = adam_part(
            left, member, unit, fit, weight, first, second, updated[name], wait_for, start, stop - start
        )
        return tick

    def reduce_step(index, level, tick):
        if level == 0:
            running[index] = [product(index, kept_rows, tick), sent[index]]
        kept, arrived = running[index]
        rows = arrived.shape[0] // 2

        def added(part):
            part = slice(part * rows, (part + 1) * rows)
            return kept[part] + arrived[part].astype(f32) + tick

        outgoing = added(1).astype(wire)
        bit = bits_of[plan[index][2]][level + 1]
        running[index] = [added(0), exchange(outgoing, 1 << bit)]
        return running[index][0]

    def total(index, tick):
        kept, arrived = running[index]
        return kept + arrived.astype(f32) + tick

    tick = update(0, wait)
    wait = [reduce_step(index, 0, tick) for index in (1, 0)]
    wait.append(send(2, tick)[:8, :128].astype(f32))
    wait.append(send(3, zero_of(wait[0]))[:8, :128].astype(f32))
    tick = update(1, wait)
    wait = [reduce_step(index, 1, tick) for index in (1, 0)]
    wait += [reduce_step(index, 0, zero_of(wait[0])) for index in (2, 3)]
    tick = update(2, wait)
    wait = [reduce_step(index, 1, tick) for index in (2, 3)]
    tick = update(3, wait)
    for level in range(2, levels - 1):
        for index in range(len(plan)):
            reduce_step(index, level, tick)
    hidden = [
        (jax.nn.silu(total(index, tick)) * total(index + 1, tick)).astype(bf16) for index in (0, 2)
    ]
    hidden = jnp.concatenate(hidden, axis=1)
    gate_new, gate_first_new, gate_second_new = updated["gate"]
    up_new, up_first_new, up_second_new = updated["up"]
    return (hidden, gate_new, up_new, gate_first_new, up_first_new, gate_second_new, up_second_new)


def solution(mesh):
    placed = (P("pop", "fsdp"), P(), P(("pop", "fsdp"))) + (P("fsdp", "pop"),) * 6
    return jax.shard_map(
        shards,
        mesh=mesh,
        in_specs=placed,
        out_specs=(P("fsdp", "pop"),) * 7,
        check_vma=False,
    )
```
